32 devices in a mesh: pipe: 2 (over x), dp: 2 (over y), tensor: 8 (over z, core).
Axes of the slice: x: 2, y: 2, z: 4, core: 2. Of those that a mesh axis runs over, the one named last changes fastest.
Arguments:
- layer_input: bfloat16 [4, 2, 1024, 1024], P(None, 'dp', 'tensor'), may hold values from -6 to 6
- segment_ids: int32 [4, 2, 1024], P(None, 'dp'), may hold values from 0 to 7, as said below
- out_cotangent: bfloat16 [4, 2, 1024, 1024], P(None, 'dp', 'tensor'), may hold values from -6 to 6
- norm_gain: float32 [2, 1024], P('pipe'), may hold values from 0.5 to 1.5
- w_zx: bfloat16 [2, 2, 1024, 2048], P('pipe', None, None, 'tensor'), may hold values from -0.1875 to 0.1875
- w_bc: bfloat16 [2, 1024, 256], P('pipe', None, 'tensor'), may hold values from -0.1875 to 0.1875
- w_dt: bfloat16 [2, 1024, 32], P('pipe', None, 'tensor'), may hold values from -0.1875 to 0.1875
- conv_x: float32 [2, 4, 2048], P('pipe', None, 'tensor'), may hold values from -0.5 to 0.5
- conv_x_bias: float32 [2, 2048], P('pipe', 'tensor'), may hold values from -0.5 to 0.5
- conv_bc: float32 [2, 4, 256], P('pipe', None, 'tensor'), may hold values from -0.5 to 0.5
- conv_bc_bias: float32 [2, 256], P('pipe', 'tensor'), may hold values from -0.5 to 0.5
- dt_bias: float32 [2, 32], P('pipe', 'tensor'), may hold values from -6 to -2
- a_log: float32 [2, 32], P('pipe', 'tensor'), may hold values from 0 to 2.77
- d_skip: float32 [2, 32], P('pipe', 'tensor'), may hold values from 0.1 to 1.9
- gate_gain: bfloat16 [2, 2048], P('pipe', 'tensor'), may hold values from 0.5 to 1.5
- w_out: bfloat16 [2, 2048, 1024], P('pipe', 'tensor'), may hold values from -0.125 to 0.125
Outputs:
- layer_outputs: bfloat16 [2, 4, 2, 1024, 1024], P('pipe', None, 'dp', 'tensor')
- input_grads: bfloat16 [2, 4, 2, 1024, 1024], P('pipe', None, 'dp', 'tensor')
- grad_norm_gain: float32 [2, 1024], P('pipe')
- grad_w_zx: float32 [2, 2, 1024, 2048], P('pipe', None, None, 'tensor')
- grad_w_bc: float32 [2, 1024, 256], P('pipe', None, 'tensor')
- grad_w_dt: float32 [2, 1024, 32], P('pipe', None, 'tensor')
- grad_conv_x: float32 [2, 4, 2048], P('pipe', None, 'tensor')
- grad_conv_x_bias: float32 [2, 2048], P('pipe', 'tensor')
- grad_conv_bc: float32 [2, 4, 256], P('pipe', None, 'tensor')
- grad_conv_bc_bias: float32 [2, 256], P('pipe', 'tensor')
- grad_dt_bias: float32 [2, 32], P('pipe', 'tensor')
- grad_a_log: float32 [2, 32], P('pipe', 'tensor')
- grad_d_skip: float32 [2, 32], P('pipe', 'tensor')
- grad_gate_gain: float32 [2, 2048], P('pipe', 'tensor')
- grad_w_out: float32 [2, 2048, 1024], P('pipe', 'tensor')
The draws below stay inside these ranges and needn't reach their ends.
Inputs may be any that keep to these rules, and one draw needn't show every extreme that they name: `segment_ids`: within each sequence the ids start at 0 and never fall; equal ids form one document. For each index of the second dimension one micro-batch, drawn from the seed, holds a single document over the whole sequence, and another reaches the largest id.
All inputs are finite; a program needn't handle non-finite values.
Results may differ from the reference program's by a relative error of at most 0.025.
Values may be sent and summed in bfloat16 or wider, within the bound.
A program may use at most 192 MiB of HBM per device.

```python
import jax
import jax.numpy as jnp
from jax import lax

D = 1024
INNER = 2048
HEADS = 32
STATE = 128
CONV = 4
BLOCK = 256
SEQ_LEN = 1024
MICRO = 4
LAYERS = 2
SEQS = 2


def draw_segment_ids(key, part):
    key = jax.random.fold_in(key, 7)
    cut_key, whole_key = jax.random.split(key)
    shape = (MICRO, SEQS, SEQ_LEN)
    cuts = jax.random.randint(cut_key, shape, 0, SEQ_LEN) < 3
    position = lax.broadcasted_iota(jnp.int32, shape, 2)
    whole_pick = jax.random.randint(whole_key, (1, SEQS, 1), 0, MICRO)
    forced_pick = (whole_pick + 1) % MICRO
    micro_ids = lax.broadcasted_iota(jnp.int32, (MICRO, SEQS, 1), 0)
    stride = SEQ_LEN // 8
    forced = jnp.logical_and(micro_ids == forced_pick, position % stride == 0)
    cuts = jnp.logical_and(jnp.logical_or(cuts, forced), position > 0)
    doc_ids = jnp.minimum(jnp.cumsum(cuts.astype(jnp.int32), axis=2), 7)
    return jnp.where(micro_ids == whole_pick, 0, doc_ids).astype(jnp.int32)


def levels(key, shape, pieces, low, high):
    def one(dim, shards_of):
        heights = jax.random.uniform(jax.random.fold_in(jax.random.fold_in(key, 6), dim), (shards_of,), jnp.float32, low / len(pieces), high / len(pieces))
        return jnp.repeat(jnp.exp(heights), shape[dim] // shards_of).reshape((-1,) + (1,) * (len(shape) - dim - 1))

    level = one(*pieces[0])
    for cut in pieces[1:]:
        level = level * one(*cut)
    return level


def bell_draw(stream_key, dims, deviation, most, cuts=(), held_as=jnp.bfloat16):
    entries = jax.random.normal(stream_key, dims, jnp.float32) * deviation
    if len(cuts) > 0:
        entries = levels(stream_key, dims, cuts, -0.22, 0.18) * entries
    return jnp.clip(entries, min=-most, max=most).astype(held_as)


def setup_inputs(seed: int = 0) -> dict:
    seeds = jax.random.split(jax.random.key(seed), 17)
    return {
        "layer_input": bell_draw(seeds[0], (MICRO, SEQS, SEQ_LEN, D), 1.0, 6.0, ((1, 2), (2, 8))),
        "segment_ids": draw_segment_ids(jax.random.fold_in(seeds[16], 71), 0),
        "out_cotangent": bell_draw(seeds[2], (MICRO, SEQS, SEQ_LEN, D), 1.0, 6.0, ((1, 2), (2, 8))),
        "norm_gain": jnp.clip(1.0 + 0.1 * jax.random.normal(seeds[3], (LAYERS, D), jnp.float32), 0.5, 1.5),
        "w_zx": bell_draw(seeds[4], (LAYERS, 2, D, INNER), D ** -0.5, 0.1875, ((0, 2), (3, 8))),
        "w_bc": bell_draw(seeds[5], (LAYERS, D, 2 * STATE), D ** -0.5, 0.1875, ((0, 2), (2, 8))),
        "w_dt": bell_draw(seeds[6], (LAYERS, D, HEADS), D ** -0.5, 0.1875, ((0, 2), (2, 8))),
        "conv_x": jnp.clip(jax.random.uniform(seeds[7], (LAYERS, CONV, INNER), jnp.float32, -0.5, 0.5) * levels(seeds[7], (LAYERS, CONV, INNER), ((0, 2), (2, 8)), -0.4, 0.0), -0.5, 0.5),
        "conv_x_bias": jnp.clip(jax.random.uniform(seeds[8], (LAYERS, INNER), jnp.float32, -0.5, 0.5) * levels(seeds[8], (LAYERS, INNER), ((0, 2), (1, 8)), -0.4, 0.0), -0.5, 0.5),
        "conv_bc": jnp.clip(jax.random.uniform(seeds[9], (LAYERS, CONV, 2 * STATE), jnp.float32, -0.5, 0.5) * levels(seeds[9], (LAYERS, CONV, 2 * STATE), ((0, 2), (2, 8)), -0.4, 0.0), -0.5, 0.5),
        "conv_bc_bias": jnp.clip(jax.random.uniform(seeds[10], (LAYERS, 2 * STATE), jnp.float32, -0.5, 0.5) * levels(seeds[10], (LAYERS, 2 * STATE), ((0, 2), (1, 8)), -0.4, 0.0), -0.5, 0.5),
        "dt_bias": jnp.clip(-6.0 + 4.0 * jax.random.uniform(seeds[11], (LAYERS, HEADS), jnp.float32) ** levels(seeds[11], (LAYERS, HEADS), ((0, 2), (1, 8)), -0.2, 0.2), -6.0, -2.0),
        "a_log": jnp.clip(2.77 * jax.random.uniform(seeds[12], (LAYERS, HEADS), jnp.float32) ** levels(seeds[12], (LAYERS, HEADS), ((0, 2), (1, 8)), -0.2, 0.2), 0.0, 2.77),
        "d_skip": jnp.clip(1.0 + 0.18 * jax.random.normal(seeds[13], (LAYERS, HEADS), jnp.float32), 0.1, 1.9),
        "gate_gain": jnp.clip(1.0 + 0.1 * jax.random.normal(seeds[14], (LAYERS, INNER), jnp.float32), 0.5, 1.5).astype(jnp.bfloat16),
        "w_out": bell_draw(seeds[15], (LAYERS, INNER, D), INNER ** -0.5, 0.125, ((0, 2), (1, 8))),
    }


EPSILON = 1e-05
PRECISE = lax.Precision.HIGHEST

@jax.custom_vjp
def low(v):
    return lax.optimization_barrier(v.astype(jnp.bfloat16)).astype(jnp.float32)

@jax.custom_vjp
def low_back(v):
    return v

def low_keep(v):
    return (low(v), None)

def low_pass(kept, grad):
    return (grad,)

def back_keep(v):
    return (v, None)

def back_low(kept, grad):
    return (low(grad),)
low.defvjp(low_keep, low_pass)
low_back.defvjp(back_keep, back_low)

def causal_conv(values, kernel, offset_bias, segments):
    taps_count = kernel.shape[0]
    length = values.shape[0]
    padded = jnp.pad(values, ((taps_count - 1, 0), (0, 0)))
    padded_ids = jnp.pad(segments, (taps_count - 1, 0), constant_values=-1)
    result = jnp.zeros_like(values) + offset_bias
    for offset in range(taps_count):
        first_row = taps_count - 1 - offset
        earlier = padded[first_row:first_row + length]
        same_doc = (padded_ids[first_row:first_row + length] == segments).astype(values.dtype)
        result = result + kernel[offset] * earlier * same_doc[:, None]
    return result

def state_scan(inputs, step_sizes, decay_rates, b_values, c_values, segments, block_size):
    length, head_count, head_width = inputs.shape
    blocks = length // block_size
    state_count = b_values.shape[1]
    log_decay = (step_sizes * decay_rates).reshape(blocks, block_size, head_count)
    cumul = jnp.cumsum(log_decay, axis=1)
    weighted = (inputs * step_sizes[:, :, None]).reshape(blocks, block_size, head_count, head_width)
    b_blocks = b_values.reshape(blocks, block_size, state_count)
    c_blocks = c_values.reshape(blocks, block_size, state_count)
    block_ids = segments.astype(jnp.int32).reshape(blocks, block_size)
    lower_mask = jnp.tril(jnp.ones((block_size, block_size), inputs.dtype))
    same_doc = (block_ids[:, :, None] == block_ids[:, None, :]).astype(inputs.dtype) * lower_mask
    cumul_heads = jnp.transpose(cumul, (0, 2, 1))
    log_gaps = cumul_heads[:, :, :, None] - cumul_heads[:, :, None, :]
    mask_heads = same_doc[:, None]
    decays = jnp.exp(jnp.where(mask_heads > 0, log_gaps, 0.0)) * mask_heads
    affinity = jnp.einsum('ctn,csn->cts', c_blocks, b_blocks, precision=PRECISE)
    inside = jnp.einsum('chts,cshp->cthp', affinity[:, None] * decays, weighted, precision=PRECISE)
    ending = cumul[:, -1, :]
    to_end = jnp.exp(ending[:, None, :] - cumul) * (block_ids == block_ids[:, -1:]).astype(inputs.dtype)[:, :, None]
    block_states = jnp.einsum('csn,cshp->chnp', b_blocks, weighted * to_end[:, :, :, None], precision=PRECISE)
    before = jnp.concatenate([jnp.full((1,), -1, jnp.int32), block_ids[:-1, -1].astype(jnp.int32)])
    carry_keep = jnp.exp(ending) * (block_ids[:, -1] == before).astype(inputs.dtype)[:, None]
    running = jnp.zeros_like(block_states[0])
    entering = []
    for block_index in range(blocks):
        entering.append(running)
        running = carry_keep[block_index][:, None, None] * running + block_states[block_index]
    entering = jnp.stack(entering)
    from_start = jnp.exp(cumul) * (block_ids == before[:, None]).astype(inputs.dtype)[:, :, None]
    across = jnp.einsum('ctn,chnp->cthp', c_blocks, entering, precision=PRECISE) * from_start[:, :, :, None]
    return (inside + across).reshape(length, head_count, head_width)

def mixer(x_proj, step_raw, bc_values, gate_raw, kernel_x, offset_x, step_bias, decay_log, skip_gain, segments, block_size):
    mixed_in = jax.nn.silu(causal_conv(x_proj, kernel_x, offset_x, segments))
    length = x_proj.shape[0]
    head_count = step_raw.shape[1]
    step_sizes = jax.nn.softplus(step_raw + step_bias)
    decay_rates = -jnp.exp(decay_log)
    state_count = bc_values.shape[1] // 2
    per_head = mixed_in.reshape(length, head_count, -1)
    scanned = state_scan(per_head, step_sizes, decay_rates, bc_values[:, :state_count], bc_values[:, state_count:], segments, block_size)
    outputs = (scanned + skip_gain[None, :, None] * per_head).reshape(length, -1)
    return outputs * jax.nn.silu(gate_raw)

def section_layer(hidden, segments, weights):
    gain_in, w_zx, w_bc, w_dt, conv_x, conv_x_bias, conv_bc, conv_bc_bias, dt_bias, a_log, d_skip, gate_gain, w_out = weights
    row_scale = lax.rsqrt(lax.optimization_barrier(jnp.mean(hidden * hidden, axis=-1, keepdims=True)) + EPSILON)
    normed = low(hidden * row_scale * gain_in)
    gate_raw = low_back(jnp.dot(normed, w_zx[0], precision=PRECISE))
    x_proj = low_back(jnp.dot(normed, w_zx[1], precision=PRECISE))
    bc_proj = low_back(jnp.dot(normed, w_bc, precision=PRECISE))
    step_raw = low_back(jnp.dot(normed, w_dt, precision=PRECISE))
    bc_values = low(jax.nn.silu(causal_conv(bc_proj, conv_bc, conv_bc_bias, segments)))
    gated = mixer(x_proj, step_raw, bc_values, gate_raw, conv_x, conv_x_bias, dt_bias, a_log, d_skip, segments, BLOCK)
    gated_scale = lax.rsqrt(lax.optimization_barrier(jnp.mean(gated * gated, axis=-1, keepdims=True)) + EPSILON)
    normed_out = low(gated * gated_scale * gate_gain)
    return hidden + jnp.dot(normed_out, w_out, precision=PRECISE)

def whole_layer(hidden, weights, segments):
    hidden = low_back(hidden)

    def one_sequence(sequence_pair):
        return jax.checkpoint(section_layer)(sequence_pair[0], sequence_pair[1], weights)
    return low(lax.map(one_sequence, (hidden, segments)))

def reference(layer_input, segment_ids, out_cotangent, norm_gain, w_zx, w_bc, w_dt, conv_x, conv_x_bias, conv_bc, conv_bc_bias, dt_bias, a_log, d_skip, gate_gain, w_out):
    seq_count = MICRO * SEQS
    hidden = layer_input.astype(jnp.float32).reshape(seq_count, SEQ_LEN, D)
    segments = segment_ids.astype(jnp.int32).reshape(seq_count, SEQ_LEN)
    stacked = (norm_gain, w_zx, w_bc, w_dt, conv_x, conv_x_bias, conv_bc, conv_bc_bias, dt_bias, a_log, d_skip, gate_gain, w_out)
    layer_weights = [tuple((weight[layer_index].astype(jnp.float32) for weight in stacked)) for layer_index in range(LAYERS)]

    def apply_layer(layer_in, weights):
        return whole_layer(layer_in, weights, segments)
    outputs = []
    pullbacks = []
    for layer_index in range(LAYERS):
        hidden, pullback = jax.vjp(apply_layer, hidden, layer_weights[layer_index])
        outputs.append(hidden)
        pullbacks.append(pullback)
    grad_flow = out_cotangent.astype(jnp.float32).reshape(seq_count, SEQ_LEN, D)
    in_grads = [None] * LAYERS
    weight_grads = [None] * LAYERS
    for layer_index in reversed(range(LAYERS)):
        grad_flow, layer_grads = pullbacks[layer_index](grad_flow)
        in_grads[layer_index] = grad_flow
        weight_grads[layer_index] = layer_grads
    full_shape = (LAYERS, MICRO, SEQS, SEQ_LEN, D)
    layer_outputs = jnp.stack(outputs).reshape(full_shape).astype(jnp.bfloat16)
    input_grads = jnp.stack(in_grads).reshape(full_shape).astype(jnp.bfloat16)
    grads = [jnp.stack([weight_grads[layer_index][number] for layer_index in range(LAYERS)]).astype(jnp.float32) for number in range(13)]
    return (layer_outputs, input_grads, grads[0], grads[1], grads[2], grads[3], grads[4], grads[5], grads[6], grads[7], grads[8], grads[9], grads[10], grads[11], grads[12])
```

```python
import jax
import jax.numpy as jnp
from jax import lax
from jax.sharding import PartitionSpec as P

BLOCK = 256


EPSILON = 1e-05
PRECISE = lax.Precision.HIGH


def causal_conv(values, kernel, offset_bias, segments):
    taps_count = kernel.shape[0]
    length = values.shape[0]
    padded = jnp.pad(values, ((taps_count - 1, 0), (0, 0)))
    padded_ids = jnp.pad(segments, (taps_count - 1, 0), constant_values=-1)
    result = jnp.zeros_like(values) + offset_bias
    for offset in range(taps_count):
        first_row = taps_count - 1 - offset
        earlier = padded[first_row : first_row + length]
        same_doc = (padded_ids[first_row : first_row + length] == segments).astype(values.dtype)
        result = result + kernel[offset] * earlier * same_doc[:, None]
    return result


def state_scan(inputs, step_sizes, decay_rates, b_values, c_values, segments, block_size):
    length, head_count, head_width = inputs.shape
    blocks = length // block_size
    state_count = b_values.shape[1]
    log_decay = (step_sizes * decay_rates).reshape(blocks, block_size, head_count)
    lower_mask = jnp.tril(jnp.ones((block_size, block_size), inputs.dtype))
    cumul = jnp.einsum(
        "ts,csh->cth", lower_mask, log_decay, precision=lax.Precision.HIGHEST
    )
    weighted = (inputs * step_sizes[:, :, None]).reshape(blocks, block_size, head_count, head_width)
    b_blocks = b_values.reshape(blocks, block_size, state_count)
    c_blocks = c_values.reshape(blocks, block_size, state_count)
    block_ids = segments.reshape(blocks, block_size)
    same_doc = (block_ids[:, :, None] == block_ids[:, None, :]).astype(inputs.dtype) * lower_mask
    cumul_heads = jnp.transpose(cumul, (0, 2, 1))
    log_gaps = cumul_heads[:, :, :, None] - cumul_heads[:, :, None, :]
    mask_heads = same_doc[:, None]
    decays = jnp.exp(jnp.where(mask_heads > 0, log_gaps, 0.0)) * mask_heads
    affinity = jnp.einsum("ctn,csn->cts", c_blocks, b_blocks)
    inside = jnp.einsum("chts,cshp->cthp", affinity[:, None] * decays, weighted, precision=PRECISE)
    ending = cumul[:, -1, :]
    to_end = (
        jnp.exp(ending[:, None, :] - cumul)
        * (block_ids == block_ids[:, -1:]).astype(inputs.dtype)[:, :, None]
    )
    block_states = jnp.einsum(
        "csn,cshp->chnp", b_blocks, weighted * to_end[:, :, :, None], precision=PRECISE
    )
    before = jnp.concatenate([jnp.full((1,), -1, jnp.int32), block_ids[:-1, -1]])
    carry_keep = jnp.exp(ending) * (block_ids[:, -1] == before).astype(inputs.dtype)[:, None]
    running = jnp.zeros_like(block_states[0])
    entering = []
    for block_index in range(blocks):
        entering.append(running)
        running = carry_keep[block_index][:, None, None] * running + block_states[block_index]
    entering = jnp.stack(entering)
    from_start = jnp.exp(cumul) * (block_ids == before[:, None]).astype(inputs.dtype)[:, :, None]
    across = (
        jnp.einsum("ctn,chnp->cthp", c_blocks, entering, precision=PRECISE)
        * from_start[:, :, :, None]
    )
    return (inside + across).reshape(length, head_count, head_width)


def mixer(
    x_proj,
    step_raw,
    bc_values,
    gate_raw,
    kernel_x,
    offset_x,
    step_bias,
    decay_log,
    skip_gain,
    segments,
    block_size,
):
    mixed_in = jax.nn.silu(causal_conv(x_proj, kernel_x, offset_x, segments))
    length = x_proj.shape[0]
    head_count = step_raw.shape[1]
    step_sizes = jax.nn.softplus(step_raw + step_bias)
    decay_rates = -jnp.exp(decay_log)
    state_count = bc_values.shape[1] // 2
    per_head = mixed_in.reshape(length, head_count, -1)
    scanned = state_scan(
        per_head,
        step_sizes,
        decay_rates,
        bc_values[:, :state_count],
        bc_values[:, state_count:],
        segments,
        block_size,
    )
    outputs = (scanned + skip_gain[None, :, None] * per_head).reshape(length, -1)
    return outputs * jax.nn.silu(gate_raw)


def bc_activate(bc_proj, kernel, offset_bias, segments):
    return jax.nn.silu(causal_conv(bc_proj, kernel, offset_bias, segments))


def local(
    layer_input,
    segment_ids,
    out_cotangent,
    norm_gain,
    w_zx,
    w_bc,
    w_dt,
    conv_x,
    conv_x_bias,
    conv_bc,
    conv_bc_bias,
    dt_bias,
    a_log,
    d_skip,
    gate_gain,
    w_out,
):
    section_count = lax.axis_size("pipe")
    section_index = lax.axis_index("pipe")
    shard_count = lax.axis_size("tensor")
    shard_index = lax.axis_index("tensor")
    micro_count = layer_input.shape[0]
    micro_local = micro_count // section_count
    row_count = layer_input.shape[2]
    model_width = layer_input.shape[3]
    inner_local = w_zx.shape[3]
    heads_local = w_dt.shape[2]
    bc_local = w_bc.shape[2]
    bc_width = bc_local * shard_count
    inner = inner_local * shard_count
    taps = conv_x.shape[1]
    first_micro = section_index * micro_local

    def mine(array):
        return lax.dynamic_slice_in_dim(array, first_micro, micro_local, 0)[:, 0]

    def sections(value):
        return lax.all_gather(value, "pipe", axis=0)

    input_rows = mine(layer_input)
    cotangent_rows = mine(out_cotangent)
    segment_rows = mine(segment_ids)

    smalls = jnp.concatenate(
        [
            norm_gain[0],
            conv_x[0].reshape(-1),
            conv_x_bias[0],
            gate_gain[0].astype(jnp.float32),
            dt_bias[0],
            a_log[0],
            d_skip[0],
        ]
    )
    smalls_all = sections(smalls)
    bc_taps = jnp.concatenate([conv_bc[0], conv_bc_bias], axis=0).T
    bc_taps_all = lax.all_gather(bc_taps, ("pipe", "tensor"), axis=0, tiled=True)
    bc_taps_all = bc_taps_all.reshape(section_count, bc_width, taps + 1)
    w_bc_all = lax.all_gather(w_bc[0].T, ("pipe", "tensor"), axis=0, tiled=True)
    w_bc_all = w_bc_all.reshape(section_count, bc_width, model_width)
    w_main = jnp.concatenate([w_zx[0, 0].T, w_zx[0, 1].T, w_out[0], w_dt[0].T], axis=0)
    w_main_all = sections(w_main)

    weights = []
    for layer in range(section_count):
        flat = smalls_all[layer]
        parts = []
        start = 0
        for size in (
            model_width,
            taps * inner_local,
            inner_local,
            inner_local,
            heads_local,
            heads_local,
            heads_local,
        ):
            parts.append(flat[start : start + size])
            start += size
        main = w_main_all[layer]
        w_cat = jnp.concatenate(
            [main[: 2 * inner_local], w_bc_all[layer], main[3 * inner_local :]], axis=0
        )
        weights.append(
            dict(
                gain_in=parts[0],
                kernel_x=parts[1].reshape(taps, inner_local),
                offset_x=parts[2],
                gain_out=parts[3],
                step_bias=parts[4],
                decay_log=parts[5],
                skip_gain=parts[6],
                kernel_bc=bc_taps_all[layer, :, :taps].T,
                offset_bc=bc_taps_all[layer, :, taps],
                w_cat=w_cat,
                w_out=main[2 * inner_local : 3 * inner_local],
            )
        )

    def own_rows(values):
        return lax.dynamic_slice_in_dim(values, shard_index * row_count, row_count, 0)

    def forward(hidden_in, segments, layer):
        w = weights[layer]
        hidden = hidden_in.astype(jnp.float32)
        row_scale = lax.rsqrt(jnp.mean(hidden * hidden, axis=-1, keepdims=True) + EPSILON)
        normed = (hidden * row_scale * w["gain_in"]).astype(jnp.bfloat16)
        gathered = lax.all_gather(normed, "tensor", axis=0, tiled=True)
        projected = lax.dot_general(
            gathered, w["w_cat"], (((1,), (1,)), ((), ())), preferred_element_type=jnp.float32
        )
        gate_raw = projected[:, :inner_local]
        x_proj = projected[:, inner_local : 2 * inner_local]
        bc_proj = projected[:, 2 * inner_local : 2 * inner_local + bc_width]
        step_raw = projected[:, 2 * inner_local + bc_width :]
        bc_values, bc_back = jax.vjp(
            lambda values, kernel, offset_bias: bc_activate(values, kernel, offset_bias, segments),
            bc_proj,
            w["kernel_bc"],
            w["offset_bc"],
        )
        bc_values = bc_values.astype(jnp.bfloat16).astype(jnp.float32)
        gated, mix_back = jax.vjp(
            lambda *values: mixer(*values, segments, BLOCK),
            x_proj,
            step_raw,
            bc_values,
            gate_raw,
            w["kernel_x"],
            w["offset_x"],
            w["step_bias"],
            w["decay_log"],
            w["skip_gain"],
        )
        squares = lax.psum(jnp.sum(gated * gated, axis=-1), "tensor")
        gated_scale = lax.rsqrt(squares / inner + EPSILON)[:, None]
        scaled = (gated * w["gain_out"]).astype(jnp.bfloat16)
        partial = jnp.dot(scaled, w["w_out"], preferred_element_type=jnp.float32)
        mixed = lax.psum_scatter(
            partial.astype(jnp.bfloat16), "tensor", scatter_dimension=0, tiled=True
        ).astype(jnp.float32)
        result = (hidden + own_rows(gated_scale) * mixed).astype(jnp.bfloat16)
        kept = (hidden_in, gathered, gated, gated_scale, mixed, bc_back, mix_back)
        return result, kept

    def backward(grad_out, grad_out_all, kept, layer):
        w = weights[layer]
        hidden_in, gathered, gated, gated_scale, mixed, bc_back, mix_back = kept
        own_dots = jnp.sum(grad_out.astype(jnp.float32) * mixed, axis=-1) / inner
        row_dots = lax.all_gather(own_dots, "tensor", axis=0, tiled=True)[:, None]
        out_grad = lax.dot_general(
            grad_out_all, w["w_out"], (((1,), (1,)), ((), ())), preferred_element_type=jnp.float32
        )
        scaled_gated = gated * gated_scale
        normed_out = (scaled_gated * w["gain_out"]).astype(jnp.bfloat16)
        weight_grad = lax.dot_general(
            normed_out, grad_out_all, (((0,), (0,)), ((), ())), preferred_element_type=jnp.float32
        )
        gain_grad = jnp.sum(out_grad * scaled_gated, axis=0)
        gated_grad = gated_scale * (out_grad * w["gain_out"]) - gated * (
            gated_scale**3 * row_dots
        )
        (
            x_grad,
            step_grad,
            bc_grad,
            gate_grad,
            kernel_x_grad,
            offset_x_grad,
            bias_grad,
            decay_grad,
            skip_grad,
        ) = mix_back(gated_grad)
        bc_proj_grad, kernel_bc_grad, offset_bc_grad = bc_back(bc_grad)
        proj_grad = jnp.concatenate([gate_grad, x_grad, bc_proj_grad, step_grad], axis=1).astype(
            jnp.bfloat16
        )
        normed_grad = lax.psum_scatter(
            jnp.dot(proj_grad, w["w_cat"], preferred_element_type=jnp.float32).astype(
                jnp.bfloat16
            ),
            "tensor",
            scatter_dimension=0,
            tiled=True,
        ).astype(jnp.float32)
        cat_grad = lax.dot_general(
            gathered, proj_grad, (((0,), (0,)), ((), ())), preferred_element_type=jnp.float32
        )
        hidden = hidden_in.astype(jnp.float32)
        row_scale = lax.rsqrt(jnp.mean(hidden * hidden, axis=-1, keepdims=True) + EPSILON)
        in_gain_grad = jnp.sum(normed_grad * hidden * row_scale, axis=0)
        scaled_in = normed_grad * w["gain_in"]
        hidden_grad = row_scale * scaled_in - hidden * row_scale**3 * jnp.mean(
            scaled_in * hidden, axis=-1, keepdims=True
        )
        grad_in = (grad_out.astype(jnp.float32) + hidden_grad).astype(jnp.bfloat16)
        local_small = jnp.concatenate(
            [
                kernel_x_grad.reshape(-1),
                offset_x_grad,
                gain_grad,
                bias_grad,
                decay_grad,
                skip_grad,
            ]
        )
        shared_small = jnp.concatenate(
            [kernel_bc_grad.reshape(-1), offset_bc_grad, in_gain_grad]
        )
        return grad_in, (cat_grad, weight_grad, local_small, shared_small)

    micros = range(micro_local)
    grads_flow = [cotangent_rows[micro] for micro in micros]
    flow = [input_rows[micro] for micro in micros]
    kept_all = []
    outputs = []
    for layer in range(section_count):
        results = [forward(flow[micro], segment_rows[micro], layer) for micro in micros]
        flow = [pair[0] for pair in results]
        kept_all.append([pair[1] for pair in results])
        outputs.append(jnp.stack(flow))
    in_grads = [None] * section_count
    totals = [None] * section_count
    for layer in reversed(range(section_count)):
        gathered_grads = [
            lax.all_gather(grads_flow[micro], "tensor", axis=0, tiled=True) for micro in micros
        ]
        results = [
            backward(grads_flow[micro], gathered_grads[micro], kept_all[layer][micro], layer)
            for micro in micros
        ]
        grads_flow = [pair[0] for pair in results]
        in_grads[layer] = jnp.stack(grads_flow)
        summed = results[0][1]
        for pair in results[1:]:
            summed = jax.tree.map(jnp.add, summed, pair[1])
        cat_grad, weight_grad, local_small, shared_small = summed
        bc_first = 2 * inner_local
        bc_sum = lax.psum_scatter(
            cat_grad[:, bc_first : bc_first + bc_width].T.astype(jnp.bfloat16),
            "tensor",
            scatter_dimension=0,
            tiled=True,
        )
        big = (
            cat_grad[:, :bc_first].astype(jnp.bfloat16),
            weight_grad.astype(jnp.bfloat16),
            jnp.concatenate(
                [bc_sum, cat_grad[:, bc_first + bc_width :].T.astype(jnp.bfloat16)], axis=0
            ),
        )
        totals[layer] = (lax.psum(big, ("pipe", "dp")), local_small, shared_small)

    def pick(values):
        chosen = values[0]
        for layer in range(1, section_count):
            chosen = jax.tree.map(
                lambda later, sooner: jnp.where(section_index == layer, later, sooner),
                values[layer],
                chosen,
            )
        return chosen

    def regroup(per_layer):
        stacked = jnp.stack(per_layer)
        moved = lax.all_to_all(stacked, "pipe", split_axis=0, concat_axis=0, tiled=True)
        return moved.reshape((micro_count,) + stacked.shape[2:])

    layer_outputs = regroup(outputs)
    input_grads = regroup(in_grads)
    zx_total, out_total, rest_total = pick([total[0] for total in totals])
    local_total = pick(lax.psum([total[1] for total in totals], ("pipe", "dp")))
    shared_total = pick(lax.psum([total[2] for total in totals], ("pipe", "dp", "tensor")))
    zx_total = zx_total.astype(jnp.float32)
    grad_zx = jnp.stack([zx_total[:, :inner_local], zx_total[:, inner_local:]])[None]
    grad_bc = rest_total[:bc_local].astype(jnp.float32).T[None]
    grad_dt = rest_total[bc_local:].astype(jnp.float32).T[None]
    pieces = []
    start = 0
    for size in (
        taps * inner_local,
        inner_local,
        inner_local,
        heads_local,
        heads_local,
        heads_local,
    ):
        pieces.append(local_total[start : start + size])
        start += size
    kernel_bc_total = shared_total[: taps * bc_width].reshape(taps, bc_width)
    offset_bc_total = shared_total[taps * bc_width : (taps + 1) * bc_width]
    norm_total = shared_total[(taps + 1) * bc_width :]
    return (
        layer_outputs[None, :, None],
        input_grads[None, :, None],
        norm_total[None],
        grad_zx,
        grad_bc,
        grad_dt,
        pieces[0].reshape(1, taps, inner_local),
        pieces[1][None],
        lax.dynamic_slice_in_dim(kernel_bc_total, shard_index * bc_local, bc_local, 1)[None],
        lax.dynamic_slice_in_dim(offset_bc_total, shard_index * bc_local, bc_local, 0)[None],
        pieces[3][None],
        pieces[4][None],
        pieces[5][None],
        pieces[2][None],
        out_total.astype(jnp.float32)[None],
    )


def solution(mesh):
    return jax.shard_map(
        local,
        mesh=mesh,
        in_specs=(
            P(None, "dp", "tensor", None),
            P(None, "dp", None),
            P(None, "dp", "tensor", None),
            P("pipe", None),
            P("pipe", None, None, "tensor"),
            P("pipe", None, "tensor"),
            P("pipe", None, "tensor"),
            P("pipe", None, "tensor"),
            P("pipe", "tensor"),
            P("pipe", None, "tensor"),
            P("pipe", "tensor"),
            P("pipe", "tensor"),
            P("pipe", "tensor"),
            P("pipe", "tensor"),
            P("pipe", "tensor"),
            P("pipe", "tensor", None),
        ),
        out_specs=(
            P("pipe", None, "dp", "tensor", None),
            P("pipe", None, "dp", "tensor", None),
            P("pipe", None),
            P("pipe", None, None, "tensor"),
            P("pipe", None, "tensor"),
            P("pipe", None, "tensor"),
            P("pipe", None, "tensor"),
            P("pipe", "tensor"),
            P("pipe", None, "tensor"),
            P("pipe", "tensor"),
            P("pipe", "tensor"),
            P("pipe", "tensor"),
            P("pipe", "tensor"),
            P("pipe", "tensor"),
            P("pipe", "tensor", None),
        ),
        check_vma=False,
    )
```

```python
import jax
import jax.numpy as jnp
from jax import lax
from jax.sharding import PartitionSpec as P

BLOCK = 256


EPSILON = 1e-05
PRECISE = lax.Precision.HIGH


def causal_conv(values, kernel, offset_bias, segments):
    taps_count = kernel.shape[0]
    length = values.shape[0]
    padded = jnp.pad(values, ((taps_count - 1, 0), (0, 0)))
    padded_ids = jnp.pad(segments, (taps_count - 1, 0), constant_values=-1)
    result = jnp.zeros_like(values) + offset_bias
    for offset in range(taps_count):
        first_row = taps_count - 1 - offset
        earlier = padded[first_row : first_row + length]
        same_doc = (padded_ids[first_row : first_row + length] == segments).astype(values.dtype)
        result = result + kernel[offset] * earlier * same_doc[:, None]
    return result


def state_scan(inputs, step_sizes, decay_rates, b_values, c_values, segments, block_size):
    length, head_count, head_width = inputs.shape
    blocks = length // block_size
    state_count = b_values.shape[1]
    log_decay = (step_sizes * decay_rates).reshape(blocks, block_size, head_count)
    lower_mask = jnp.tril(jnp.ones((block_size, block_size), inputs.dtype))
    cumul = jnp.einsum(
        "ts,csh->cth", lower_mask, log_decay, precision=lax.Precision.HIGHEST
    )
    weighted = (inputs * step_sizes[:, :, None]).reshape(blocks, block_size, head_count, head_width)
    b_blocks = b_values.reshape(blocks, block_size, state_count)
    c_blocks = c_values.reshape(blocks, block_size, state_count)
    block_ids = segments.reshape(blocks, block_size)
    same_doc = (block_ids[:, :, None] == block_ids[:, None, :]).astype(inputs.dtype) * lower_mask
    cumul_heads = jnp.transpose(cumul, (0, 2, 1))
    log_gaps = cumul_heads[:, :, :, None] - cumul_heads[:, :, None, :]
    mask_heads = same_doc[:, None]
    decays = jnp.exp(jnp.where(mask_heads > 0, log_gaps, 0.0)) * mask_heads
    affinity = jnp.einsum("ctn,csn->cts", c_blocks, b_blocks)
    inside = jnp.einsum("chts,cshp->cthp", affinity[:, None] * decays, weighted, precision=PRECISE)
    ending = cumul[:, -1, :]
    to_end = (
        jnp.exp(ending[:, None, :] - cumul)
        * (block_ids == block_ids[:, -1:]).astype(inputs.dtype)[:, :, None]
    )
    block_states = jnp.einsum(
        "csn,cshp->chnp", b_blocks, weighted * to_end[:, :, :, None], precision=PRECISE
    )
    before = jnp.concatenate([jnp.full((1,), -1, jnp.int32), block_ids[:-1, -1]])
    carry_keep = jnp.exp(ending) * (block_ids[:, -1] == before).astype(inputs.dtype)[:, None]
    running = jnp.zeros_like(block_states[0])
    entering = []
    for block_index in range(blocks):
        entering.append(running)
        running = carry_keep[block_index][:, None, None] * running + block_states[block_index]
    entering = jnp.stack(entering)
    from_start = jnp.exp(cumul) * (block_ids == before[:, None]).astype(inputs.dtype)[:, :, None]
    across = (
        jnp.einsum("ctn,chnp->cthp", c_blocks, entering, precision=PRECISE)
        * from_start[:, :, :, None]
    )
    return (inside + across).reshape(length, head_count, head_width)


def mixer(
    x_proj,
    step_raw,
    bc_values,
    gate_raw,
    kernel_x,
    offset_x,
    step_bias,
    decay_log,
    skip_gain,
    segments,
    block_size,
):
    mixed_in = jax.nn.silu(causal_conv(x_proj, kernel_x, offset_x, segments))
    length = x_proj.shape[0]
    head_count = step_raw.shape[1]
    step_sizes = jax.nn.softplus(step_raw + step_bias)
    decay_rates = -jnp.exp(decay_log)
    state_count = bc_values.shape[1] // 2
    per_head = mixed_in.reshape(length, head_count, -1)
    scanned = state_scan(
        per_head,
        step_sizes,
        decay_rates,
        bc_values[:, :state_count],
        bc_values[:, state_count:],
        segments,
        block_size,
    )
    outputs = (scanned + skip_gain[None, :, None] * per_head).reshape(length, -1)
    return outputs * jax.nn.silu(gate_raw)


def bc_activate(bc_proj, kernel, offset_bias, segments):
    return jax.nn.silu(causal_conv(bc_proj, kernel, offset_bias, segments))


def local(
    layer_input,
    segment_ids,
    out_cotangent,
    norm_gain,
    w_zx,
    w_bc,
    w_dt,
    conv_x,
    conv_x_bias,
    conv_bc,
    conv_bc_bias,
    dt_bias,
    a_log,
    d_skip,
    gate_gain,
    w_out,
):
    section_count = lax.axis_size("pipe")
    section_index = lax.axis_index("pipe")
    shard_count = lax.axis_size("tensor")
    shard_index = lax.axis_index("tensor")
    micro_count = layer_input.shape[0]
    micro_local = micro_count // section_count
    row_count = layer_input.shape[2]
    model_width = layer_input.shape[3]
    inner_local = w_zx.shape[3]
    heads_local = w_dt.shape[2]
    bc_local = w_bc.shape[2]
    bc_width = bc_local * shard_count
    inner = inner_local * shard_count
    taps = conv_x.shape[1]
    first_micro = section_index * micro_local

    def mine(array):
        return lax.dynamic_slice_in_dim(array, first_micro, micro_local, 0)[:, 0]

    def sections(value):
        return lax.all_gather(value, "pipe", axis=0)

    input_rows = mine(layer_input)
    cotangent_rows = mine(out_cotangent)
    segment_rows = mine(segment_ids)

    smalls = jnp.concatenate(
        [
            norm_gain[0],
            conv_x[0].reshape(-1),
            conv_x_bias[0],
            gate_gain[0].astype(jnp.float32),
            dt_bias[0],
            a_log[0],
            d_skip[0],
        ]
    )
    smalls_all = sections(smalls)
    left = jnp.concatenate([conv_bc[0], conv_bc_bias], axis=0).T
    terms = []
    for _ in range(3):
        term = lax.reduce_precision(left, 8, 7)
        terms.append(term.astype(jnp.bfloat16))
        left = left - term
    filler = jnp.zeros((bc_local, 128 - 3 * (taps + 1)), jnp.bfloat16)
    bc_pack = jnp.concatenate([w_bc[0].T] + terms + [filler], axis=1)
    bc_all = lax.all_gather(bc_pack, ("pipe", "tensor"), axis=0, tiled=True)
    bc_all = bc_all.reshape(section_count, bc_width, model_width + 128)
    w_bc_all = bc_all[:, :, :model_width]
    taps_terms = bc_all[:, :, model_width : model_width + 3 * (taps + 1)].astype(jnp.float32)
    bc_taps_all = jnp.sum(taps_terms.reshape(section_count, bc_width, 3, taps + 1), axis=2)
    w_main = jnp.concatenate([w_zx[0, 0].T, w_zx[0, 1].T, w_dt[0].T], axis=0)
    w_main_all = sections(w_main)
    w_out_all = sections(w_out[0])

    weights = []
    for layer in range(section_count):
        flat = smalls_all[layer]
        parts = []
        start = 0
        for size in (
            model_width,
            taps * inner_local,
            inner_local,
            inner_local,
            heads_local,
            heads_local,
            heads_local,
        ):
            parts.append(flat[start : start + size])
            start += size
        main = w_main_all[layer]
        w_cat = jnp.concatenate(
            [main[: 2 * inner_local], w_bc_all[layer], main[2 * inner_local :]], axis=0
        )
        weights.append(
            dict(
                gain_in=parts[0],
                kernel_x=parts[1].reshape(taps, inner_local),
                offset_x=parts[2],
                gain_out=parts[3],
                step_bias=parts[4],
                decay_log=parts[5],
                skip_gain=parts[6],
                kernel_bc=bc_taps_all[layer, :, :taps].T,
                offset_bc=bc_taps_all[layer, :, taps],
                w_cat=w_cat,
                w_out=w_out_all[layer],
            )
        )

    def own_rows(values):
        return lax.dynamic_slice_in_dim(values, shard_index * row_count, row_count, 0)

    def forward(hidden_in, segments, layer, order):
        w = weights[layer]
        hidden = hidden_in.astype(jnp.float32)
        row_scale = lax.rsqrt(jnp.mean(hidden * hidden, axis=-1, keepdims=True) + EPSILON)
        normed = (hidden * row_scale * w["gain_in"]).astype(jnp.bfloat16)
        gathered = lax.all_gather(normed, "tensor", axis=0, tiled=True)
        projected = lax.dot_general(
            gathered, w["w_cat"], (((1,), (1,)), ((), ())), preferred_element_type=jnp.float32
        )
        gate_raw = projected[:, :inner_local]
        x_proj = projected[:, inner_local : 2 * inner_local]
        bc_proj = projected[:, 2 * inner_local : 2 * inner_local + bc_width]
        step_raw = projected[:, 2 * inner_local + bc_width :]
        bc_values, bc_back = jax.vjp(
            lambda values, kernel, offset_bias: bc_activate(values, kernel, offset_bias, segments),
            bc_proj,
            w["kernel_bc"] + order,
            w["offset_bc"],
        )
        bc_values = bc_values.astype(jnp.bfloat16).astype(jnp.float32)
        gated, mix_back = jax.vjp(
            lambda *values: mixer(*values, segments, BLOCK),
            x_proj,
            step_raw,
            bc_values,
            gate_raw,
            w["kernel_x"] + order,
            w["offset_x"],
            w["step_bias"],
            w["decay_log"],
            w["skip_gain"],
        )
        squares = lax.psum(jnp.sum(gated * gated, axis=-1), "tensor")
        gated_scale = lax.rsqrt(squares / inner + EPSILON)[:, None]
        scaled = (gated * w["gain_out"]).astype(jnp.bfloat16)
        partial = jnp.dot(scaled, w["w_out"], preferred_element_type=jnp.float32)
        mixed = lax.psum_scatter(
            partial.astype(jnp.bfloat16), "tensor", scatter_dimension=0, tiled=True
        ).astype(jnp.float32)
        result = (hidden + own_rows(gated_scale) * mixed).astype(jnp.bfloat16)
        kept = (hidden_in, gathered, gated, gated_scale, mixed, bc_back, mix_back)
        return result, kept, 0.0 * (partial[0, 0] + squares[0])

    def backward(grad_out, grad_out_all, row_dots, kept, layer, order):
        w = weights[layer]
        hidden_in, gathered, gated, gated_scale, mixed, bc_back, mix_back = kept
        out_grad = lax.dot_general(
            grad_out_all, w["w_out"], (((1,), (1,)), ((), ())), preferred_element_type=jnp.float32
        )
        scaled_gated = gated * gated_scale
        normed_out = (scaled_gated * w["gain_out"]).astype(jnp.bfloat16)
        weight_grad = lax.dot_general(
            normed_out, grad_out_all, (((0,), (0,)), ((), ())), preferred_element_type=jnp.float32
        )
        gain_grad = jnp.sum(out_grad * scaled_gated, axis=0)
        gated_grad = gated_scale * (out_grad * (w["gain_out"] + order)) - gated * (
            gated_scale**3 * row_dots
        )
        (
            x_grad,
            step_grad,
            bc_grad,
            gate_grad,
            kernel_x_grad,
            offset_x_grad,
            bias_grad,
            decay_grad,
            skip_grad,
        ) = mix_back(gated_grad)
        bc_proj_grad, kernel_bc_grad, offset_bc_grad = bc_back(bc_grad)
        proj_grad = jnp.concatenate([gate_grad, x_grad, bc_proj_grad, step_grad], axis=1).astype(
            jnp.bfloat16
        )
        spread_grad = jnp.dot(proj_grad, w["w_cat"], preferred_element_type=jnp.float32)
        normed_grad = lax.psum_scatter(
            spread_grad.astype(jnp.bfloat16),
            "tensor",
            scatter_dimension=0,
            tiled=True,
        ).astype(jnp.float32)
        cat_grad = lax.dot_general(
            gathered, proj_grad, (((0,), (0,)), ((), ())), preferred_element_type=jnp.float32
        )
        hidden = hidden_in.astype(jnp.float32)
        row_scale = lax.rsqrt(jnp.mean(hidden * hidden, axis=-1, keepdims=True) + EPSILON)
        in_gain_grad = jnp.sum(normed_grad * hidden * row_scale, axis=0)
        scaled_in = normed_grad * w["gain_in"]
        hidden_grad = row_scale * scaled_in - hidden * row_scale**3 * jnp.mean(
            scaled_in * hidden, axis=-1, keepdims=True
        )
        grad_in = (grad_out.astype(jnp.float32) + hidden_grad).astype(jnp.bfloat16)
        local_small = jnp.concatenate(
            [
                kernel_x_grad.reshape(-1),
                offset_x_grad,
                gain_grad,
                bias_grad,
                decay_grad,
                skip_grad,
            ]
        )
        shared_small = jnp.concatenate(
            [kernel_bc_grad.reshape(-1), offset_bc_grad, in_gain_grad]
        )
        order = 0.0 * spread_grad[0, 0]
        return grad_in, (cat_grad, weight_grad, local_small, shared_small), order

    def dots_of(grad_out, kept):
        return jnp.sum(grad_out.astype(jnp.float32) * kept[4], axis=-1) / inner

    micros = range(micro_local)
    grads_flow = [cotangent_rows[micro] for micro in micros]
    flow = [input_rows[micro] for micro in micros]
    kept_all = []
    outputs = []
    order = jnp.float32(0.0)
    for layer in range(section_count):
        results = []
        for micro in micros:
            results.append(forward(flow[micro], segment_rows[micro], layer, order))
            order = results[-1][2]
        flow = [pair[0] for pair in results]
        kept_all.append([pair[1] for pair in results])
        outputs.append(jnp.stack(flow))
    in_grads = [None] * section_count
    totals = [None] * section_count
    for layer in reversed(range(section_count)):
        gathered_grads = [
            lax.all_gather(grads_flow[micro], "tensor", axis=0, tiled=True) for micro in micros
        ]
        if layer == section_count - 1:
            own_dots = jnp.stack(
                [dots_of(grads_flow[micro], kept_all[layer][micro]) for micro in micros]
            )
            dots_all = lax.all_gather(own_dots, "tensor", axis=1, tiled=True)
            row_dots = [dots_all[micro][:, None] for micro in micros]
        else:
            row_dots = [
                lax.all_gather(
                    dots_of(grads_flow[micro], kept_all[layer][micro]),
                    "tensor",
                    axis=0,
                    tiled=True,
                )[:, None]
                for micro in micros
            ]
        results = []
        for micro in micros:
            results.append(
                backward(
                    grads_flow[micro],
                    gathered_grads[micro],
                    row_dots[micro],
                    kept_all[layer][micro],
                    layer,
                    order,
                )
            )
            order = results[-1][2]
        grads_flow = [pair[0] for pair in results]
        in_grads[layer] = jnp.stack(grads_flow)
        summed = results[0][1]
        for pair in results[1:]:
            summed = jax.tree.map(jnp.add, summed, pair[1])
        cat_grad, weight_grad, local_small, shared_small = summed
        bc_first = 2 * inner_local
        small_rows = -(-local_small.size // model_width)
        bc_sum = lax.psum_scatter(
            cat_grad[:, bc_first : bc_first + bc_width].T.astype(jnp.bfloat16),
            "tensor",
            scatter_dimension=0,
            tiled=True,
        )
        big = (
            cat_grad[:, :bc_first].astype(jnp.bfloat16),
            weight_grad.astype(jnp.bfloat16),
            jnp.concatenate(
                [
                    bc_sum,
                    cat_grad[:, bc_first + bc_width :].T.astype(jnp.bfloat16),
                    jnp.pad(local_small, (0, small_rows * model_width - local_small.size))
                    .reshape(small_rows, model_width)
                    .astype(jnp.bfloat16),
                ],
                axis=0,
            ),
        )
        if layer < section_count - 1:
            zero = 0.0 * totals[layer + 1][0][2][0, 0]
            big = jax.tree.map(lambda value: value + zero, big)
        totals[layer] = (lax.psum(big, ("pipe", "dp")), shared_small)

    def pick(values):
        chosen = values[0]
        for layer in range(1, section_count):
            chosen = jax.tree.map(
                lambda later, sooner: jnp.where(section_index == layer, later, sooner),
                values[layer],
                chosen,
            )
        return chosen

    def regroup(per_layer):
        stacked = jnp.stack(per_layer)
        moved = lax.all_to_all(stacked, "pipe", split_axis=0, concat_axis=0, tiled=True)
        return moved.reshape((micro_count,) + stacked.shape[2:])

    layer_outputs = regroup(outputs)
    input_grads = regroup(in_grads)
    zx_total, out_total, rest_total = pick([total[0] for total in totals])
    local_total = rest_total[bc_local + heads_local :].astype(jnp.float32).reshape(-1)
    shared_total = pick(lax.psum([total[1] for total in totals], ("pipe", "dp", "tensor")))
    zx_total = zx_total.astype(jnp.float32)
    grad_zx = jnp.stack([zx_total[:, :inner_local], zx_total[:, inner_local:]])[None]
    grad_bc = rest_total[:bc_local].astype(jnp.float32).T[None]
    grad_dt = rest_total[bc_local : bc_local + heads_local].astype(jnp.float32).T[None]
    pieces = []
    start = 0
    for size in (
        taps * inner_local,
        inner_local,
        inner_local,
        heads_local,
        heads_local,
        heads_local,
    ):
        pieces.append(local_total[start : start + size])
        start += size
    kernel_bc_total = shared_total[: taps * bc_width].reshape(taps, bc_width)
    offset_bc_total = shared_total[taps * bc_width : (taps + 1) * bc_width]
    norm_total = shared_total[(taps + 1) * bc_width :]
    return (
        layer_outputs[None, :, None],
        input_grads[None, :, None],
        norm_total[None],
        grad_zx,
        grad_bc,
        grad_dt,
        pieces[0].reshape(1, taps, inner_local),
        pieces[1][None],
        lax.dynamic_slice_in_dim(kernel_bc_total, shard_index * bc_local, bc_local, 1)[None],
        lax.dynamic_slice_in_dim(offset_bc_total, shard_index * bc_local, bc_local, 0)[None],
        pieces[3][None],
        pieces[4][None],
        pieces[5][None],
        pieces[2][None],
        out_total.astype(jnp.float32)[None],
    )


def solution(mesh):
    return jax.shard_map(
        local,
        mesh=mesh,
        in_specs=(
            P(None, "dp", "tensor", None),
            P(None, "dp", None),
            P(None, "dp", "tensor", None),
            P("pipe", None),
            P("pipe", None, None, "tensor"),
            P("pipe", None, "tensor"),
            P("pipe", None, "tensor"),
            P("pipe", None, "tensor"),
            P("pipe", "tensor"),
            P("pipe", None, "tensor"),
            P("pipe", "tensor"),
            P("pipe", "tensor"),
            P("pipe", "tensor"),
            P("pipe", "tensor"),
            P("pipe", "tensor"),
            P("pipe", "tensor", None),
        ),
        out_specs=(
            P("pipe", None, "dp", "tensor", None),
            P("pipe", None, "dp", "tensor", None),
            P("pipe", None),
            P("pipe", None, None, "tensor"),
            P("pipe", None, "tensor"),
            P("pipe", None, "tensor"),
            P("pipe", None, "tensor"),
            P("pipe", "tensor"),
            P("pipe", None, "tensor"),
            P("pipe", "tensor"),
            P("pipe", "tensor"),
            P("pipe", "tensor"),
            P("pipe", "tensor"),
            P("pipe", "tensor"),
            P("pipe", "tensor", None),
        ),
        check_vma=False,
    )
```
